512 devices in a mesh: group: 16 (over x_lo, z), dev: 32 (over x_hi, y, core).
Axes of the slice: x: 4 (x_hi: 2, x_lo: 2; x = x_hi * 2 + x_lo), y: 8, z: 8, core: 2. Of those that a mesh axis runs over, the one named last changes fastest.
Arguments:
- patches: bfloat16 [16, 32, 256, 1152], P('group', 'dev'), may hold values from -6 to 6
- norm_gain: float32 [1152], replicated, may hold values from 0.1 to 1.9
- kv_weight: bfloat16 [4096, 1152], P(('group', 'dev')), may hold values from -0.1875 to 0.1875
- latent_q: bfloat16 [64, 2048], replicated
- clip_frames: int32 [16, 32], P('group', 'dev'), may hold values from 1 to 8, as said below
- row_owner: int32 [16, 32, 256], P('group', 'dev'), may hold values from 0 to 31, as said below
- row_slot: int32 [16, 32, 256], P('group', 'dev'), may hold values from 0 to 15, as said below
- slot_pos: int32 [16, 32, 512], P('group', 'dev'), may hold values from 0 to 512, as said below
- latent_blocks: int32 [16, 32, 64, 2], P('group', 'dev'), may hold values from -1 to 3, as said below
Outputs:
- latent_out: bfloat16 [2048, 32768], P('dev', 'group')
The draws below stay inside these ranges and needn't reach their ends.
Inputs may be any that keep to these rules, and one draw needn't show every extreme that they name: `clip_frames`: A group's clips hold 4 * 32 frames together; every group has a clip of 8 frames and one of 2 frames or fewer. `row_owner`: A device holds exactly f * 2 rows of each clip of its group that has f frames. `row_slot`: the rows that one device holds for one clip carry the slots 0, 1, and so on, each once. `slot_pos`: for a clip of f frames the entries s * 16 + k, with k below the number of rows of that clip on device s, name the positions 0 to f * 64 - 1 each once; every other entry is 512. `latent_blocks`: for a clip of b = ceil(f / 2) blocks, entry 0 of latent i is block i * b // 64; entry 1 is a block beside it, or -1 where b is 1.
All inputs are finite; a program needn't handle non-finite values.
Results may differ from the reference program's by a relative error of at most 0.0055.
The reference program's roundings to bfloat16 on the way (of `normed`, `keyval`, `timeline` and `attn_weights`) count: a program that leaves them out, or rounds other values in their place, can miss the bound.
Values may be sent and summed in bfloat16 or wider, within the bound.
A program may use at most 64 MiB of HBM per device.

```python
import jax
import jax.numpy as jnp
import numpy as np
from jax import lax

V = 1152
HD = 128
LAT = 64
FR_ROWS = 64
HW = 2048
CAP = 512
SLOT = 16
SRC = 256
N_GROUP = 16
N_DEV = 32


frame_table = np.array([[8, 4, 2, 2], [8, 1, 3, 4], [5, 5, 3, 3], [4, 4, 4, 4], [7, 6, 2, 1], [6, 5, 4, 1], [3, 3, 7, 3], [2, 8, 5, 1]], np.int32)


def group_layout(group_key):
    subkeys = jax.random.split(group_key, 5)
    quad_count = N_DEV // 4
    picked = jax.random.randint(subkeys[0], (quad_count,), 0, 8).at[0].set(0)
    pattern = jnp.asarray(frame_table)[picked].reshape(N_DEV)
    frames = pattern[jax.random.permutation(subkeys[1], N_DEV)].astype(jnp.int32)
    group_rows = 4 * N_DEV * FR_ROWS
    per_sender = FR_ROWS // N_DEV
    lengths = frames * FR_ROWS
    clip_ends = jnp.cumsum(lengths)
    clip_starts = clip_ends - lengths
    row_index = jnp.arange(group_rows, dtype=jnp.int32)
    owners = jnp.sum((row_index[:, None] >= clip_ends[None, :]).astype(jnp.int32), axis=1)
    positions = row_index - clip_starts[owners]
    frame_keys = jax.random.split(subkeys[2], 4 * N_DEV)
    spreads = jax.vmap(lambda frame_key: jax.random.permutation(frame_key, FR_ROWS))(frame_keys)
    sender = (spreads.reshape(-1) // per_sender).astype(jnp.int32)
    tiebreak = jax.random.permutation(subkeys[3], group_rows).astype(jnp.int32)
    sorted_order = jnp.argsort(sender * group_rows + tiebreak, stable=True)
    owner_rows = owners[sorted_order].reshape(N_DEV, SRC)
    place_rows = positions[sorted_order].reshape(N_DEV, SRC)
    onehot = (owner_rows[:, :, None] == jnp.arange(N_DEV, dtype=jnp.int32)[None, None, :]).astype(jnp.int32)
    slot_rank = jnp.sum(jnp.cumsum(onehot, axis=1) * onehot, axis=2) - 1
    source = jnp.arange(N_DEV, dtype=jnp.int32)[:, None] * jnp.ones((1, SRC), jnp.int32)
    slot_table = jnp.full((N_DEV, CAP), CAP, jnp.int32).at[owner_rows, source * SLOT + slot_rank].set(place_rows)
    blocks = (frames + 1) // 2
    centre = jnp.arange(LAT, dtype=jnp.int32)[None, :] * blocks[:, None] // LAT
    offset_side = jax.random.randint(subkeys[4], (N_DEV, LAT), 0, 2) * 2 - 1
    second = centre + offset_side
    second = jnp.where(second >= blocks[:, None], centre - 1, second)
    second = jnp.where(second < 0, centre + 1, second)
    second = jnp.where(blocks[:, None] == 1, -1, second)
    listed = jnp.stack([centre, second], axis=-1).astype(jnp.int32)
    return (frames, owner_rows.astype(jnp.int32), slot_rank.astype(jnp.int32), slot_table, listed)


def layout_all(key):
    base_key = jax.random.fold_in(key, 7)
    return jax.vmap(group_layout)(jax.random.split(base_key, N_GROUP))


def draw_clip_frames(key, part):
    return layout_all(key)[0]


def draw_row_owner(key, part):
    return layout_all(key)[1]


def draw_row_slot(key, part):
    return layout_all(key)[2]


def draw_slot_pos(key, part):
    return layout_all(key)[3]


def draw_latent_blocks(key, part):
    return layout_all(key)[4]


def draw_latent_q(key, part):
    normal_part = jnp.clip(jax.random.normal(key, (LAT, HW), jnp.float32), -4.0, 4.0)
    return (3.0 * normal_part).astype(jnp.bfloat16)


def steps_of(key, shape, cuts, low, largest):
    level = 1.0
    for axis_at, shards_of in cuts:
        heights = jax.random.uniform(jax.random.fold_in(jax.random.fold_in(key, 6), axis_at), (shards_of,), jnp.float32, low / len(cuts), largest / len(cuts))
        level = level * jnp.repeat(jnp.exp(heights), shape[axis_at] // shards_of).reshape((-1,) + (1,) * (len(shape) - 1 - axis_at))
    return level


def gaussian(own_key, dims, scale, limit, pieces=(), kind=jnp.bfloat16):
    values = jax.random.normal(own_key, dims, jnp.float32) * scale
    if len(pieces) > 0:
        values = steps_of(own_key, dims, pieces, -0.22, 0.18) * values
    return jnp.clip(values, min=-limit, max=limit).astype(kind)


def setup_inputs(seed: int = 0) -> dict:
    streams_of = jax.random.split(jax.random.key(seed), 10)
    patches = gaussian(streams_of[0], (N_GROUP, N_DEV, SRC, V), 1.0, 6.0, ((0, 16), (1, 32)))
    norm_gain = jnp.clip(1.0 + 0.18 * jax.random.normal(streams_of[1], (V,), jnp.float32), 0.1, 1.9)
    kv_weight = gaussian(streams_of[2], (2 * HW, V), V ** -0.5, 0.1875, ((0, 512),))
    latent_q = draw_latent_q(jax.random.fold_in(streams_of[9], 71), 0)
    clip_frames = draw_clip_frames(jax.random.fold_in(streams_of[9], 71), 0)
    row_owner = draw_row_owner(jax.random.fold_in(streams_of[9], 71), 0)
    row_slot = draw_row_slot(jax.random.fold_in(streams_of[9], 71), 0)
    slot_pos = draw_slot_pos(jax.random.fold_in(streams_of[9], 71), 0)
    latent_blocks = draw_latent_blocks(jax.random.fold_in(streams_of[9], 71), 0)
    return dict(patches=patches, norm_gain=norm_gain, kv_weight=kv_weight, latent_q=latent_q, clip_frames=clip_frames, row_owner=row_owner, row_slot=row_slot, slot_pos=slot_pos, latent_blocks=latent_blocks)


def rms_rows(patch_rows, norm_gain):
    widened = patch_rows.astype(jnp.float32)
    inverse_rms = lax.rsqrt(lax.optimization_barrier(jnp.mean(widened * widened, axis=-1, keepdims=True)) + 1e-06)
    return (widened * inverse_rms * norm_gain).astype(jnp.bfloat16)

def attend(keyval, frames, listed, latent_q):
    capacity = keyval.shape[0]
    kv_width = keyval.shape[1] // 2
    head_count = kv_width // HD
    key_part = keyval[:, :kv_width].reshape(capacity, head_count, HD).astype(jnp.float32)
    value_part = keyval[:, kv_width:].reshape(capacity, head_count, HD).astype(jnp.float32)
    queries = latent_q.reshape(LAT, head_count, HD).astype(jnp.float32)
    scores = jnp.einsum('ihd,jhd->hij', queries, key_part) * HD ** (-0.5)
    position = jnp.arange(capacity, dtype=jnp.int32)
    block_id = position // (2 * FR_ROWS)
    allowed = ((block_id[None, :] == listed[:, 0:1]) | (block_id[None, :] == listed[:, 1:2])) & (position[None, :] < frames * FR_ROWS)
    scores = jnp.where(allowed[None, :, :], scores, jnp.float32(-1e+30))
    row_max = lax.optimization_barrier(jnp.max(scores, axis=-1, keepdims=True))
    raised = jnp.exp(scores - row_max)
    row_sum = lax.optimization_barrier(jnp.sum(raised, axis=-1, keepdims=True))
    attn_weights = (raised / row_sum).astype(jnp.bfloat16).astype(jnp.float32)
    blended = jnp.einsum('hij,jhd->hdi', attn_weights, value_part)
    return blended.astype(jnp.bfloat16).reshape(kv_width, LAT)

def reference(patches, norm_gain, kv_weight, latent_q, clip_frames, row_owner, row_slot, slot_pos, latent_blocks):

    def one_group(group_data):
        held_rows, frames, owners, slot_ids, places, listed = group_data
        normed = rms_rows(held_rows.reshape(N_DEV * SRC, V), norm_gain)
        keyval = jnp.dot(normed, kv_weight.T, preferred_element_type=jnp.float32).astype(jnp.bfloat16)
        sender = jnp.repeat(jnp.arange(N_DEV, dtype=jnp.int32), SRC)
        flat_owner = owners.reshape(-1).astype(jnp.int32)
        target = places[flat_owner, sender * SLOT + slot_ids.reshape(-1).astype(jnp.int32)].astype(jnp.int32)
        timeline = jnp.zeros((N_DEV * CAP, 2 * HW), jnp.bfloat16).at[flat_owner * CAP + target].set(keyval)
        timeline = timeline.reshape(N_DEV, CAP, 2 * HW)
        blended = lax.map(lambda clip_data: attend(clip_data[0], clip_data[1], clip_data[2], latent_q), (timeline, frames, listed))
        return jnp.transpose(blended, (1, 0, 2)).reshape(HW, N_DEV * LAT)
    gathered = lax.map(one_group, (patches, clip_frames, row_owner, row_slot, slot_pos, latent_blocks))
    return jnp.transpose(gathered, (1, 0, 2)).reshape(HW, N_GROUP * N_DEV * LAT)
```

```python
import jax
import jax.numpy as jnp
from jax import lax
from jax.experimental import pallas as pl
from jax.experimental.pallas import tpu as pltpu
from jax.sharding import PartitionSpec as P

HD = 128
LAT = 64
FR_ROWS = 64
V = 1152
COLS_A = 640
COLS_B = 512
CAP = 512
SLOT = 16
NX, NY, NZ = 4, 8, 8
CHIPS = 16
MESH = pl.DeviceIdType.MESH
F32 = jnp.float32
BF16 = jnp.bfloat16


def device_at(x, y, z, core):
    return ((x % 2) * NZ + z, (x // 2) * 2 * NY + y * 2 + core)


def slab_at(x, z):
    return ((x % 2) * NZ + z) * 2 + x // 2


def offsets(n):
    found = [0]
    for step in range(1, n // 2):
        found += [step, -step]
    return found + [n // 2]


def nt_dot(left, right):
    return lax.dot_general(left, right, (((1,), (1,)), ((), ())), preferred_element_type=F32)


def remote(src, dst, send_sem, recv_sem, target):
    return pltpu.make_async_remote_copy(
        src_ref=src,
        dst_ref=dst,
        send_sem=send_sem,
        recv_sem=recv_sem,
        device_id=target,
        device_id_type=MESH,
    )


def kernel(
    patches,
    gain,
    weight,
    queries,
    frames,
    owner,
    slot,
    places,
    listed,
    out,
    part_a,
    part_b,
    rows,
    outbox,
    wide,
    masks,
    packed,
    pair_s,
    pair_r,
    ring_y_s,
    ring_y_r,
    first_s,
    first_r,
    second_s,
    second_r,
    swap_s,
    swap_r,
    send_s,
    send_r,
    hand_s,
    hand_r,
    mask_s,
    mask_r,
    out_s,
    out_r,
):
    group = lax.axis_index("group")
    dev = lax.axis_index("dev")
    x_lo, z = group // NZ, group % NZ
    x_hi, in_line = dev // (2 * NY), dev % (2 * NY)
    y, core = in_line // 2, in_line % 2
    x = x_hi * 2 + x_lo
    chip = dev // 2
    sibling = (group, chip * 2 + 1 - core)

    barrier = pltpu.get_barrier_semaphore()

    def greet(offset, carry):
        pl.semaphore_signal(
            barrier, inc=1, device_id=(group, (dev + offset) % 32), device_id_type=MESH
        )
        return carry

    lax.fori_loop(1, 32, greet, 0)
    for target in (
        device_at(x, y, (z + 1) % NZ, core),
        device_at(x, y, (z + NZ - 1) % NZ, core),
        device_at((x + 1) % NX, y, z, core),
        device_at((x + NX - 1) % NX, y, z, core),
    ):
        pl.semaphore_signal(barrier, inc=1, device_id=target, device_id_type=MESH)
    pl.semaphore_wait(barrier, 35)

    wide[core] = weight[...].astype(F32)
    pair = remote(wide.at[core], wide.at[core], pair_s, pair_r, sibling)
    pair.start()

    position = places[...]
    block_id = position // (2 * FR_ROWS)
    marks = listed[...]
    allowed = ((block_id == marks[:, 0:1]) | (block_id == marks[:, 1:2])) & (
        position < frames[...] * FR_ROWS
    )
    masks[core] = jnp.where(allowed, F32(1.0), F32(0.0))
    mask_copy = remote(masks.at[core], masks.at[core], mask_s, mask_r, sibling)
    mask_copy.start()
    pair.wait_recv()

    chip_rows = pl.ds(pl.multiple_of(y * 16, 16), 16)
    mine = slab_at(x, z)

    def spread(part, low, high):
        both = jnp.concatenate([wide[0, :, low:high], wide[1, :, low:high]], axis=0)
        part[mine, chip_rows, :] = both.astype(BF16)
        for offset in range(1, NY):
            along_y(part, offset).start()

    def along_y(part, offset):
        block = part.at[mine, chip_rows, :]
        return remote(
            block,
            block,
            ring_y_s.at[offset],
            ring_y_r.at[offset],
            device_at(x, (y + offset) % NY, z, core),
        )

    @pl.when(core == 0)
    def _():
        spread(part_a, 0, COLS_A)

    @pl.when(core == 1)
    def _():
        spread(part_b, COLS_A, V)

    widened = patches[...].astype(F32)
    inverse_rms = lax.rsqrt(jnp.sum(widened * widened, axis=-1, keepdims=True) * (1.0 / V) + 1e-06)
    normed = (widened * inverse_rms * gain[...]).astype(BF16)
    target_slot = owner[...] * SLOT + slot[...]
    onehot = (
        lax.broadcasted_iota(jnp.int32, (CAP, target_slot.shape[1]), 0) == target_slot
    ).astype(F32).astype(BF16)
    outbox[...] = (
        jnp.dot(onehot, normed, preferred_element_type=F32).astype(BF16).reshape(CHIPS, 2, SLOT, V)
    )

    own_rows = pl.ds(pl.multiple_of(dev * SLOT, SLOT), SLOT)

    def dispatch(offset):
        there = (chip + offset) % CHIPS
        return remote(
            outbox.at[there],
            rows.at[:, own_rows, :],
            send_s.at[offset],
            send_r.at[offset],
            (group, there * 2 + core),
        )

    def hand_over(offset):
        source = (chip + CHIPS - offset) % CHIPS
        block = rows.at[:, pl.ds(pl.multiple_of((source * 2 + core) * SLOT, SLOT), SLOT), :]
        return remote(block, block, hand_s.at[offset], hand_r.at[offset], sibling)

    def start_dispatch(offset, carry):
        dispatch(offset).start()
        return carry

    lax.fori_loop(1, CHIPS, start_dispatch, 0)
    rows[:, own_rows, :] = outbox[chip]
    hand_over(0).start()

    def gather(part, n1, at1, n2, at2, slab_of, device_of):
        offs = offsets(n1)
        half1, half2 = n1 // 2, n2 // 2

        def first(k, j, way):
            place = (at1 - way * k + n1) % n1
            block = part.at[slab_of(place, at2), pl.ds(j * 64, 64), :]
            index = ((way + 1) // 2 * half1 + k) * 2 + j
            return remote(
                block,
                block,
                first_s.at[index],
                first_r.at[index],
                device_of((at1 + way + n1) % n1, at2),
            )

        def second(k, t, way):
            place = (at2 - way * k + n2) % n2
            block = part.at[slab_of((at1 + offs[t] + n1) % n1, place)]
            index = ((way + 1) // 2 * half2 + k) * n1 + t
            return remote(
                block,
                block,
                second_s.at[index],
                second_r.at[index],
                device_of(at1, (at2 + way + n2) % n2),
            )

        return first, second, half1, half2, offs

    def swap(part, sx, sz):
        index = (sx % 2) * NZ + sz
        block = part.at[slab_at(sx, sz)]
        return remote(block, block, swap_s.at[index], swap_r.at[index], sibling)

    def run_gather(part, n1, at1, n2, at2, slab_of, device_of, xz_of, other):
        first, second, half1, half2, offs = gather(part, n1, at1, n2, at2, slab_of, device_of)

        def landed(t, place2):
            sx, sz = xz_of((at1 + offs[t] + n1) % n1, place2)

            @pl.when(sx // 2 == other)
            def _():
                swap(part, sx, sz).start()

        def complete(t):
            second(0, t, 1).start()
            second(0, t, -1).start()
            landed(t, at2)

        for offset in range(1, NY):
            along_y(part, offset).wait_recv()
        for j in range(2):
            for way in (1, -1):
                first(0, j, way).start()
        complete(0)
        for k in range(1, half1 + 1):
            for way in (-1, 1):
                for j in range(2):
                    last = k == half1
                    if last and j != (1 - way) // 2:
                        continue
                    first(k - 1, j, way).wait_recv()
                    if k < half1 - 1 or (k == half1 - 1 and j == (1 - way) // 2):
                        first(k, j, way).start()
                if k < half1:
                    complete(2 * k if way == 1 else 2 * k - 1)
        complete(n1 - 1)
        for k in range(1, half2 + 1):
            for t in range(n1):
                for way in (1, -1):
                    chosen = t % 2 == (1 - way) // 2
                    if k == half2 and not chosen:
                        continue
                    second(k - 1, t, way).wait_recv()
                    if k < half2 - 1 or (k == half2 - 1 and chosen):
                        second(k, t, way).start()
                    landed(t, (at2 - way * k + n2) % n2)

    def end_gather(part, n1, at1, n2, at2, slab_of, device_of):
        first, second, half1, half2, offs = gather(part, n1, at1, n2, at2, slab_of, device_of)
        for offset in range(1, NY):
            along_y(part, offset).wait_send()
        for way in (1, -1):
            for k in range(half1):
                for j in range(2):
                    if k < half1 - 1 or j == (1 - way) // 2:
                        first(k, j, way).wait_send()
            for k in range(half2):
                for t in range(n1):
                    if k < half2 - 1 or t % 2 == (1 - way) // 2:
                        second(k, t, way).wait_send()

    plan_a = (
        part_a,
        NX,
        x,
        NZ,
        z,
        lambda a, b: slab_at(a, b),
        lambda a, b: device_at(a, y, b, core),
    )
    plan_b = (
        part_b,
        NZ,
        z,
        NX,
        x,
        lambda a, b: slab_at(b, a),
        lambda a, b: device_at(b, y, a, core),
    )

    @pl.when(core == 0)
    def _():
        run_gather(*plan_a, lambda a, b: (a, b), 1)

    @pl.when(core == 1)
    def _():
        run_gather(*plan_b, lambda a, b: (b, a), 0)

    def hand_all(offset, carry):
        source = (chip + CHIPS - offset) % CHIPS
        block = rows.at[:, pl.ds(pl.multiple_of((source * 2 + core) * SLOT, SLOT), SLOT), :]
        remote(block, block, send_s.at[offset], send_r.at[offset], sibling).wait_recv()
        hand_over(offset).start()
        return carry

    lax.fori_loop(1, CHIPS, hand_all, 0)
    mask_copy.wait_recv()

    def hand_wait(offset, carry):
        hand_over(offset).wait_recv()
        return carry

    lax.fori_loop(0, CHIPS, hand_wait, 0)

    def swap_wait_a(index, carry):
        swap(part_b, index // NZ, index % NZ).wait_recv()
        return carry

    def swap_wait_b(index, carry):
        swap(part_a, 2 + index // NZ, index % NZ).wait_recv()
        return carry

    @pl.when(core == 0)
    def _():
        lax.fori_loop(0, 16, swap_wait_a, 0)

    @pl.when(core == 1)
    def _():
        lax.fori_loop(0, 16, swap_wait_b, 0)

    chip_cols = pl.ds(pl.multiple_of(chip * 128, 128), 128)

    def result(step, half):
        head = 2 * ((y + step) % NZ) + core
        target = 2 * head + half
        copy = remote(
            packed.at[step, pl.ds(half * 64, 64), :],
            out.at[:, chip_cols],
            out_s.at[2 * step + half],
            out_r.at[chip],
            (group, target),
        )
        return target, copy

    def attend(step, carry):
        head = 2 * ((y + step) % NZ) + core
        left = jnp.concatenate([part_a[head], part_a[16 + head]], axis=0)
        right = jnp.concatenate([part_b[head], part_b[16 + head]], axis=0)
        query = queries[:, pl.ds(pl.multiple_of(head * HD, HD), HD)]
        blended = []
        for clip in range(2):
            keyval = (
                nt_dot(rows[clip, :, 0:COLS_A], left) + nt_dot(rows[clip, :, COLS_A:V], right)
            ).astype(BF16)
            scores = nt_dot(query, keyval[:, :HD]) * HD ** (-0.5)
            scores = jnp.where(masks[clip] > 0.5, scores, F32(-1e30))
            raised = jnp.exp(scores - jnp.max(scores, axis=-1, keepdims=True))
            weights = (raised / jnp.sum(raised, axis=-1, keepdims=True)).astype(BF16)
            blended.append(jnp.dot(weights, keyval[:, HD:], preferred_element_type=F32))
        packed[step] = jnp.concatenate(blended, axis=0).T.astype(BF16)
        for half in range(2):
            target, copy = result(step, half)

            @pl.when(target == dev)
            def _():
                out[:, chip_cols] = packed[step, half * 64 : (half + 1) * 64, :]

            @pl.when(target != dev)
            def _():
                copy.start()

        return carry

    lax.fori_loop(0, NZ, attend, 0)

    def finish(offset, carry):
        source = (chip + CHIPS - offset) % CHIPS
        from_dev = source * 2 + (y % 2)

        @pl.when(from_dev != dev)
        def _():
            block = out.at[:, pl.ds(pl.multiple_of(source * 128, 128), 128)]
            remote(
                packed.at[0, pl.ds(0, 64), :], block, out_s.at[0], out_r.at[source], sibling
            ).wait_recv()

        return carry

    lax.fori_loop(0, CHIPS, finish, 0)

    def sent(step, carry):
        for half in range(2):
            target, copy = result(step, half)

            @pl.when(target != dev)
            def _():
                copy.wait_send()

        return carry

    lax.fori_loop(0, NZ, sent, 0)

    pair.wait_send()
    mask_copy.wait_send()

    def sent_rows(offset, carry):
        dispatch(offset).wait_send()
        return carry

    lax.fori_loop(1, CHIPS, sent_rows, 0)

    def handed(offset, carry):
        hand_over(offset).wait_send()
        return carry

    lax.fori_loop(0, CHIPS, handed, 0)

    def swapped_a(index, carry):
        swap(part_a, 2 + index // NZ, index % NZ).wait_send()
        return carry

    def swapped_b(index, carry):
        swap(part_b, index // NZ, index % NZ).wait_send()
        return carry

    @pl.when(core == 0)
    def _():
        end_gather(*plan_a)
        lax.fori_loop(0, 16, swapped_a, 0)

    @pl.when(core == 1)
    def _():
        end_gather(*plan_b)
        lax.fori_loop(0, 16, swapped_b, 0)


def per_device(
    patches,
    norm_gain,
    kv_weight,
    latent_q,
    clip_frames,
    row_owner,
    row_slot,
    slot_pos,
    latent_blocks,
):
    vmem = pl.BlockSpec(memory_space=pltpu.VMEM)
    dma = pltpu.SemaphoreType.DMA
    scratch = [
        pltpu.VMEM((32, HD, COLS_A), BF16),
        pltpu.VMEM((32, HD, COLS_B), BF16),
        pltpu.VMEM((2, CAP, V), BF16),
        pltpu.VMEM((CHIPS, 2, SLOT, V), BF16),
        pltpu.VMEM((2, 8, V), F32),
        pltpu.VMEM((2, LAT, CAP), F32),
        pltpu.VMEM((8, HD, 2 * LAT), BF16),
    ]
    scratch += [dma, dma]
    for count in (8, 16, 32, 16, 16, 16):
        scratch += [dma((count,)), dma((count,))]
    scratch += [dma, dma, dma((16,)), dma((16,))]
    return pl.pallas_call(
        kernel,
        out_shape=jax.ShapeDtypeStruct((64, 2048), BF16),
        in_specs=[vmem] * 9,
        out_specs=vmem,
        scratch_shapes=scratch,
        compiler_params=pltpu.CompilerParams(
            collective_id=0, has_side_effects=True, vmem_limit_bytes=48 * 1024 * 1024
        ),
    )(
        patches[0, 0],
        norm_gain.reshape(1, V),
        kv_weight,
        latent_q,
        clip_frames,
        row_owner[0],
        row_slot[0],
        slot_pos[0],
        latent_blocks[0, 0],
    )


def solution(mesh):
    return jax.shard_map(
        per_device,
        mesh=mesh,
        in_specs=(
            P("group", "dev", None, None),
            P(),
            P(("group", "dev"), None),
            P(),
            P("group", "dev"),
            P("group", "dev", None),
            P("group", "dev", None),
            P("group", "dev", None),
            P("group", "dev", None, None),
        ),
        out_specs=P("dev", "group"),
        check_vma=False,
    )
```

```python
import jax
import jax.numpy as jnp
from jax import lax
from jax.experimental import pallas as pl
from jax.experimental.pallas import tpu as pltpu
from jax.sharding import PartitionSpec as P

HD = 128
LAT = 64
FR_ROWS = 64
V = 1152
COLS_A = 512
COLS_B = 640
CAP = 512
SLOT = 16
NX, NY, NZ = 4, 8, 8
CHIPS = 16
MESH = pl.DeviceIdType.MESH
F32 = jnp.float32
BF16 = jnp.bfloat16


def device_at(x, y, z, core):
    return ((x % 2) * NZ + z, (x // 2) * 2 * NY + y * 2 + core)


def slab_at(x, z):
    return ((x % 2) * NZ + z) * 2 + x // 2


def offsets(n):
    found = [0]
    for step in range(1, n // 2):
        found += [step, -step]
    return found + [n // 2]


ORDER = [o + y for y in (4, 3, 5, 2, 6, 1, 7, 0) for o in (0, 8) if o + y > 0]
FIRST, EVERY, LAG = 15, 1, 24
EARLY_A, EARLY_B = 2, 0


def nt_dot(left, right):
    return lax.dot_general(left, right, (((1,), (1,)), ((), ())), preferred_element_type=F32)


def softmax(scores, mask):
    scores = jnp.where(mask > 0.5, scores * HD ** (-0.5), F32(-1e30))
    raised = jnp.exp(scores - jnp.max(scores, axis=-1, keepdims=True))
    return (raised * (1.0 / jnp.sum(raised, axis=-1, keepdims=True))).astype(BF16)


def remote(src, dst, send_sem, recv_sem, target):
    return pltpu.make_async_remote_copy(
        src_ref=src,
        dst_ref=dst,
        send_sem=send_sem,
        recv_sem=recv_sem,
        device_id=target,
        device_id_type=MESH,
    )


def kernel(
    patches,
    gain,
    weight,
    queries,
    frames,
    owner,
    slot,
    places,
    listed,
    out,
    part_a,
    part_b,
    rows,
    outbox,
    wide,
    masks,
    packed,
    pair_s,
    pair_r,
    ring_y_s,
    ring_y_r,
    first_s,
    first_r,
    second_s,
    second_r,
    swap_s,
    swap_r,
    send_s,
    send_r,
    hand_s,
    hand_r,
    mask_s,
    mask_r,
    out_s,
    out_r,
):
    group = lax.axis_index("group")
    dev = lax.axis_index("dev")
    x_lo, z = group // NZ, group % NZ
    x_hi, in_line = dev // (2 * NY), dev % (2 * NY)
    y, core = in_line // 2, in_line % 2
    x = x_hi * 2 + x_lo
    chip = dev // 2
    sibling = (group, chip * 2 + 1 - core)

    barrier = pltpu.get_barrier_semaphore()

    def greet(offset, carry):
        pl.semaphore_signal(
            barrier, inc=1, device_id=(group, (dev + offset) % 32), device_id_type=MESH
        )
        return carry

    lax.fori_loop(1, 32, greet, 0)
    for target in (
        device_at(x, y, (z + 1) % NZ, core),
        device_at(x, y, (z + NZ - 1) % NZ, core),
        device_at((x + 1) % NX, y, z, core),
        device_at((x + NX - 1) % NX, y, z, core),
    ):
        pl.semaphore_signal(barrier, inc=1, device_id=target, device_id_type=MESH)
    pl.semaphore_wait(barrier, 35)

    wide[core] = weight[...].astype(F32)
    pair = remote(wide.at[core], wide.at[core], pair_s, pair_r, sibling)
    pair.start()

    position = places[...]
    block_id = position // (2 * FR_ROWS)
    marks = listed[...]
    allowed = ((block_id == marks[:, 0:1]) | (block_id == marks[:, 1:2])) & (
        position < frames[...] * FR_ROWS
    )
    masks[core] = jnp.where(allowed, F32(1.0), F32(0.0))
    mask_copy = remote(masks.at[core], masks.at[core], mask_s, mask_r, sibling)
    mask_copy.start()
    pair.wait_recv()

    chip_rows = pl.ds(pl.multiple_of(y * 16, 16), 16)
    mine = slab_at(x, z)

    def spread(part, low, high):
        both = jnp.concatenate([wide[0, :, low:high], wide[1, :, low:high]], axis=0)
        part[mine, chip_rows, :] = both.astype(BF16)
        for offset in range(1, NY):
            along_y(part, offset).start()

    def along_y(part, offset):
        block = part.at[mine, chip_rows, :]
        return remote(
            block,
            block,
            ring_y_s.at[offset],
            ring_y_r.at[offset],
            device_at(x, (y + offset) % NY, z, core),
        )

    @pl.when(core == 0)
    def _():
        spread(part_a, 0, COLS_A)

    @pl.when(core == 1)
    def _():
        spread(part_b, COLS_A, V)

    widened = patches[...].astype(F32)
    inverse_rms = lax.rsqrt(jnp.sum(widened * widened, axis=-1, keepdims=True) * (1.0 / V) + 1e-06)
    normed = (widened * inverse_rms * gain[...]).astype(BF16)
    target_slot = owner[...] * SLOT + slot[...]
    onehot = (
        lax.broadcasted_iota(jnp.int32, (CAP, target_slot.shape[1]), 0) == target_slot
    ).astype(F32).astype(BF16)
    outbox[...] = (
        jnp.dot(onehot, normed, preferred_element_type=F32).astype(BF16).reshape(CHIPS, 2, SLOT, V)
    )

    def chip_off(offset, way):
        return (chip // 8 + offset // 8) % 2 * 8 + (chip + way * offset + 16) % 8

    own_rows = pl.ds(pl.multiple_of(dev * SLOT, SLOT), SLOT)

    def dispatch(offset):
        there = chip_off(offset, 1)
        return remote(
            outbox.at[there],
            rows.at[:, own_rows, :],
            send_s.at[offset],
            send_r.at[offset],
            (group, there * 2 + core),
        )

    def hand_over(offset):
        source = chip_off(offset, -1)
        block = rows.at[:, pl.ds(pl.multiple_of((source * 2 + core) * SLOT, SLOT), SLOT), :]
        return remote(block, block, hand_s.at[offset], hand_r.at[offset], sibling)

    rows[:, own_rows, :] = outbox[chip]
    hand_over(0).start()

    def gather(part, n1, at1, n2, at2, slab_of, device_of):
        offs = offsets(n1)
        half1, half2 = n1 // 2, n2 // 2

        def first(k, j, way):
            place = (at1 - way * k + n1) % n1
            block = part.at[slab_of(place, at2), pl.ds(j * 64, 64), :]
            index = ((way + 1) // 2 * half1 + k) * 2 + j
            return remote(
                block,
                block,
                first_s.at[index],
                first_r.at[index],
                device_of((at1 + way + n1) % n1, at2),
            )

        def second(k, t, way):
            place = (at2 - way * k + n2) % n2
            block = part.at[slab_of((at1 + offs[t] + n1) % n1, place)]
            index = ((way + 1) // 2 * half2 + k) * n1 + t
            return remote(
                block,
                block,
                second_s.at[index],
                second_r.at[index],
                device_of(at1, (at2 + way + n2) % n2),
            )

        return first, second, half1, half2, offs

    def swap(part, sx, sz):
        index = (sx % 2) * NZ + sz
        block = part.at[slab_at(sx, sz)]
        return remote(block, block, swap_s.at[index], swap_r.at[index], sibling)

    def hand_one(offset):
        dispatch(offset).wait_recv()
        hand_over(offset).start()

    chip_cols = pl.ds(pl.multiple_of(chip * 128, 128), 128)

    def head_of(step):
        return 2 * ((z + NZ + (step + 1) // 2 * (2 * (step % 2) - 1)) % NZ) + core

    def result(step, half):
        target = 2 * head_of(step) + half
        copy = remote(
            packed.at[step, pl.ds(half * 64, 64), :],
            out.at[:, chip_cols],
            out_s.at[2 * step + half],
            out_r.at[chip],
            (group, target),
        )
        return target, copy

    def attend(lowest, count):
        heads = [head_of(lowest + i) for i in range(count)]
        blocks, scored = [], []
        for head in heads:
            both = jnp.concatenate(
                [
                    jnp.concatenate([part_a[head], part_a[16 + head]], axis=0),
                    jnp.concatenate([part_b[head], part_b[16 + head]], axis=0),
                ],
                axis=1,
            )
            blocks.append([nt_dot(both, rows[clip]).astype(BF16) for clip in range(2)])
        for i, head in enumerate(heads):
            query = queries[:, pl.ds(pl.multiple_of(head * HD, HD), HD)]
            scored.append(
                [jnp.dot(query, part[:HD], preferred_element_type=F32) for part in blocks[i]]
            )
        weights = [[softmax(one[clip], masks[clip]) for clip in range(2)] for one in scored]
        for i in range(count):
            packed[lowest + i] = jnp.concatenate(
                [nt_dot(blocks[i][clip][HD:], weights[i][clip]) for clip in range(2)], axis=1
            ).astype(BF16)
        for i in range(count):
            for half in range(2):
                send_result(lowest + i, half)

    def send_result(step, half):
        target, copy = result(step, half)

        @pl.when(target == dev)
        def _():
            out[:, chip_cols] = packed[step, half * 64 : (half + 1) * 64, :]

        @pl.when(target != dev)
        def _():
            copy.start()

    def attend_pairs(other_part, low, high):
        def pair_of_heads(u, carry):
            for i in range(2):
                place = head_of(2 * u + i) // 2
                for half in range(2):
                    swap(other_part, 2 * core + half, place).wait_recv()
            attend(2 * u, 2)
            return carry

        lax.fori_loop(low, high, pair_of_heads, 0)

    def hand_wait(offset, carry):
        hand_over(offset).wait_recv()
        return carry

    def run_gather(part, n1, at1, n2, at2, slab_of, device_of, xz_of, other, other_part, early):
        first, second, half1, half2, offs = gather(part, n1, at1, n2, at2, slab_of, device_of)

        def landed(t, place2):
            sx, sz = xz_of((at1 + offs[t] + n1) % n1, place2)

            @pl.when(sx // 2 == other)
            def _():
                swap(part, sx, sz).start()

        def complete(t):
            second(0, t, 1).start()
            second(0, t, -1).start()
            landed(t, at2)

        state = [0, 0, 0]

        def tick():
            state[0] += 1
            while state[1] < len(ORDER) and state[1] < FIRST + (state[0] - 1) / EVERY:
                dispatch(ORDER[state[1]]).start()
                state[1] += 1
            while state[2] < len(ORDER) and state[2] < FIRST + (state[0] - 1 - LAG) / EVERY:
                hand_one(ORDER[state[2]])
                state[2] += 1

        for offset in range(1, NY):
            along_y(part, offset).wait_recv()
        for j in range(2):
            for way in (1, -1):
                first(0, j, way).start()
        complete(0)
        tick()
        for k in range(1, half1 + 1):
            for way in (-1, 1):
                for j in range(2):
                    last = k == half1
                    if last and j != (1 - way) // 2:
                        continue
                    first(k - 1, j, way).wait_recv()
                    if k < half1 - 1 or (k == half1 - 1 and j == (1 - way) // 2):
                        first(k, j, way).start()
                if k < half1:
                    complete(2 * k if way == 1 else 2 * k - 1)
                    tick()
        complete(n1 - 1)
        tick()
        for k in range(1, half2 + 1):
            if k == half2:
                for offset in ORDER[state[1] :]:
                    dispatch(offset).start()
                for offset in ORDER[state[2] :]:
                    hand_one(offset)
                mask_copy.wait_recv()
                lax.fori_loop(0, CHIPS, hand_wait, 0)
                attend_pairs(other_part, 0, early)
            for t in range(n1):
                for way in (1, -1):
                    chosen = t % 2 == (1 - way) // 2
                    if k == half2 and not chosen:
                        continue
                    second(k - 1, t, way).wait_recv()
                    if k < half2 - 1 or (k == half2 - 1 and chosen):
                        second(k, t, way).start()
                    landed(t, (at2 - way * k + n2) % n2)
                    if k < half2:
                        tick()
        attend_pairs(other_part, early, NZ // 2)

    def end_gather(part, n1, at1, n2, at2, slab_of, device_of):
        first, second, half1, half2, offs = gather(part, n1, at1, n2, at2, slab_of, device_of)
        for offset in range(1, NY):
            along_y(part, offset).wait_send()
        for way in (1, -1):
            for k in range(half1):
                for j in range(2):
                    if k < half1 - 1 or j == (1 - way) // 2:
                        first(k, j, way).wait_send()
            for k in range(half2):
                for t in range(n1):
                    if k < half2 - 1 or t % 2 == (1 - way) // 2:
                        second(k, t, way).wait_send()

    plan_a = (
        part_a,
        NX,
        x,
        NZ,
        z,
        lambda a, b: slab_at(a, b),
        lambda a, b: device_at(a, y, b, core),
    )
    plan_b = (
        part_b,
        NZ,
        z,
        NX,
        x,
        lambda a, b: slab_at(b, a),
        lambda a, b: device_at(b, y, a, core),
    )

    @pl.when(core == 0)
    def _():
        run_gather(*plan_a, lambda a, b: (a, b), 1, part_b, EARLY_A)

    @pl.when(core == 1)
    def _():
        run_gather(*plan_b, lambda a, b: (b, a), 0, part_a, EARLY_B)

    def finish(offset, carry):
        source = (chip + CHIPS - offset) % CHIPS
        from_dev = source * 2 + (y % 2)

        @pl.when(from_dev != dev)
        def _():
            block = out.at[:, pl.ds(pl.multiple_of(source * 128, 128), 128)]
            remote(
                packed.at[0, pl.ds(0, 64), :], block, out_s.at[0], out_r.at[source], sibling
            ).wait_recv()

        return carry

    lax.fori_loop(0, CHIPS, finish, 0)

    def sent(step, carry):
        for half in range(2):
            target, copy = result(step, half)

            @pl.when(target != dev)
            def _():
                copy.wait_send()

        return carry

    lax.fori_loop(0, NZ, sent, 0)

    pair.wait_send()
    mask_copy.wait_send()

    def sent_rows(offset, carry):
        dispatch(offset).wait_send()
        return carry

    lax.fori_loop(1, CHIPS, sent_rows, 0)

    def handed(offset, carry):
        hand_over(offset).wait_send()
        return carry

    lax.fori_loop(0, CHIPS, handed, 0)

    def swapped_a(index, carry):
        swap(part_a, 2 + index // NZ, index % NZ).wait_send()
        return carry

    def swapped_b(index, carry):
        swap(part_b, index // NZ, index % NZ).wait_send()
        return carry

    @pl.when(core == 0)
    def _():
        end_gather(*plan_a)
        lax.fori_loop(0, 16, swapped_a, 0)

    @pl.when(core == 1)
    def _():
        end_gather(*plan_b)
        lax.fori_loop(0, 16, swapped_b, 0)


def per_device(
    patches,
    norm_gain,
    kv_weight,
    latent_q,
    clip_frames,
    row_owner,
    row_slot,
    slot_pos,
    latent_blocks,
):
    vmem = pl.BlockSpec(memory_space=pltpu.VMEM)
    dma = pltpu.SemaphoreType.DMA
    scratch = [
        pltpu.VMEM((32, HD, COLS_A), BF16),
        pltpu.VMEM((32, HD, COLS_B), BF16),
        pltpu.VMEM((2, CAP, V), BF16),
        pltpu.VMEM((CHIPS, 2, SLOT, V), BF16),
        pltpu.VMEM((2, 8, V), F32),
        pltpu.VMEM((2, LAT, CAP), F32),
        pltpu.VMEM((8, HD, 2 * LAT), BF16),
    ]
    scratch += [dma, dma]
    for count in (8, 16, 32, 16, 16, 16):
        scratch += [dma((count,)), dma((count,))]
    scratch += [dma, dma, dma((16,)), dma((16,))]
    return pl.pallas_call(
        kernel,
        out_shape=jax.ShapeDtypeStruct((64, 2048), BF16),
        in_specs=[vmem] * 9,
        out_specs=vmem,
        scratch_shapes=scratch,
        compiler_params=pltpu.CompilerParams(
            collective_id=0, has_side_effects=True, vmem_limit_bytes=48 * 1024 * 1024
        ),
    )(
        patches[0, 0],
        norm_gain.reshape(1, V),
        kv_weight,
        latent_q,
        clip_frames,
        row_owner[0],
        row_slot[0],
        slot_pos[0],
        latent_blocks[0, 0],
    )


def solution(mesh):
    return jax.shard_map(
        per_device,
        mesh=mesh,
        in_specs=(
            P("group", "dev", None, None),
            P(),
            P(("group", "dev"), None),
            P(),
            P("group", "dev"),
            P("group", "dev", None),
            P("group", "dev", None),
            P("group", "dev", None),
            P("group", "dev", None, None),
        ),
        out_specs=P("dev", "group"),
        check_vma=False,
    )
```

```python
import jax
import jax.numpy as jnp
from jax import lax
from jax.experimental import pallas as pl
from jax.experimental.pallas import tpu as pltpu
from jax.sharding import PartitionSpec as P

HD = 128
LAT = 64
FR_ROWS = 64
V = 1152
COLS_A = 640
COLS_B = 512
CAP = 512
SLOT = 16
NX, NY, NZ = 4, 8, 8
MESH = pl.DeviceIdType.MESH
F32 = jnp.float32
BF16 = jnp.bfloat16


def device_at(x, y, z, core):
    return ((x % 2) * NZ + z, (x // 2) * 2 * NY + y * 2 + core)


def slab_at(x, z):
    return ((x % 2) * NZ + z) * 2 + x // 2


ORDER = (1, 7, 2, 6, 3, 5, 4)
ROWS_AT = {
    0: ((1, 7), ()),
    2: ((), (0,)),
    3: ((2, 6), ()),
    5: ((), (1, 7)),
    7: ((3, 5), ()),
    8: ((), (2, 6)),
    11: ((4,), ()),
    12: ((), (3, 5)),
}
FIRST = (1, 7)


def nt_dot(left, right):
    return lax.dot_general(left, right, (((1,), (1,)), ((), ())), preferred_element_type=F32)


def softmax(scores, mask):
    scores = jnp.where(mask > 0.5, scores * HD ** (-0.5), F32(-1e30))
    raised = jnp.exp(scores - jnp.max(scores, axis=-1, keepdims=True))
    return (raised * (1.0 / jnp.sum(raised, axis=-1, keepdims=True))).astype(BF16)


def remote(src, dst, send_sem, recv_sem, target):
    return pltpu.make_async_remote_copy(
        src_ref=src,
        dst_ref=dst,
        send_sem=send_sem,
        recv_sem=recv_sem,
        device_id=target,
        device_id_type=MESH,
    )


def kernel(
    patches_far,
    gain,
    weight,
    queries_far,
    frames,
    owner,
    slot,
    places,
    listed,
    out,
    part_a,
    part_b,
    rows,
    outbox,
    wide,
    meta,
    masks,
    packed,
    patches,
    queries,
    near_s,
    pair_s,
    pair_r,
    ring_y_s,
    ring_y_r,
    first_s,
    first_r,
    second_s,
    second_r,
    swap_s,
    swap_r,
    send_s,
    send_r,
    cross_s,
    cross_r,
    hand_s,
    hand_r,
    meta_s,
    meta_r,
    out_s,
    out_r,
):
    group = lax.axis_index("group")
    dev = lax.axis_index("dev")
    x_lo, z = group // NZ, group % NZ
    x_hi, in_line = dev // (2 * NY), dev % (2 * NY)
    y, core = in_line // 2, in_line % 2
    x = x_hi * 2 + x_lo
    sibling = (group, x_hi * 2 * NY + y * 2 + 1 - core)
    partner = (group, (1 - x_hi) * 2 * NY + y * 2 + core)
    partner_sibling = (group, (1 - x_hi) * 2 * NY + y * 2 + 1 - core)
    beside = ((1 - x_lo) * NZ + z, dev)

    near = [
        pltpu.make_async_copy(patches_far, patches, near_s.at[0]),
        pltpu.make_async_copy(queries_far, queries, near_s.at[1]),
    ]
    for copy in near:
        copy.start()

    barrier = pltpu.get_barrier_semaphore()

    def greet(offset, carry):
        pl.semaphore_signal(
            barrier, inc=1, device_id=(group, (dev + offset) % 32), device_id_type=MESH
        )
        return carry

    lax.fori_loop(1, 32, greet, 0)
    for target in (
        device_at(x, y, (z + 1) % NZ, core),
        device_at(x, y, (z + NZ - 1) % NZ, core),
        beside,
    ):
        pl.semaphore_signal(barrier, inc=1, device_id=target, device_id_type=MESH)
    own_rows = pl.ds(pl.multiple_of(dev * SLOT, SLOT), SLOT)

    def rows_of(x_hi_from, offset):
        source = x_hi_from * 2 * NY + (y + NY - offset) % NY * 2 + core
        return rows.at[:, :, pl.ds(pl.multiple_of(source * SLOT, SLOT), SLOT), :]

    def dispatch(offset):
        there = (y + offset) % NY
        return remote(
            outbox.at[:, there],
            rows.at[:, :, own_rows, :],
            send_s.at[offset],
            send_r.at[offset],
            (group, x_hi * 2 * NY + there * 2 + core),
        )

    def cross(offset):
        block = rows_of(x_hi, offset)
        return remote(block, block, cross_s.at[offset], cross_r.at[offset], partner)

    def hand_over(far, offset):
        block = rows_of(1 - x_hi if far else x_hi, offset)
        index = far * NY + offset
        return remote(block, block, hand_s.at[index], hand_r.at[index], sibling)

    near[0].wait()
    widened = patches[...].astype(F32)
    inverse_rms = lax.rsqrt(jnp.sum(widened * widened, axis=-1, keepdims=True) * (1.0 / V) + 1e-06)
    normed = (widened * inverse_rms * gain[...].reshape(1, V)).astype(BF16)
    target_slot = owner[...] * SLOT + slot[...]
    onehot = (
        lax.broadcasted_iota(jnp.int32, (CAP, target_slot.shape[1]), 0) == target_slot
    ).astype(F32).astype(BF16)
    outbox[...] = (
        jnp.dot(onehot, normed, preferred_element_type=F32).astype(BF16).reshape(2, NY, 2, SLOT, V)
    )
    rows[:, :, own_rows, :] = outbox[:, y]
    pl.semaphore_wait(barrier, 34)

    cross(0).start()
    hand_over(0, 0).start()
    for offset in FIRST:
        dispatch(offset).start()

    wide[core] = weight[...].astype(F32)
    pair = remote(wide.at[core], wide.at[core], pair_s, pair_r, sibling)
    pair.start()

    position = places[...]
    marks = listed[...]
    block_of = lax.broadcasted_iota(jnp.int32, (8, CAP), 0)
    in_block = (block_of == position // (2 * FR_ROWS)) & (position < frames[...] * FR_ROWS)
    named = lax.broadcasted_iota(jnp.int32, (8, LAT), 0)
    named = (named == marks[0:1, :]) | (named == marks[1:2, :])
    meta[x_hi, core, :, 0:CAP] = jnp.where(in_block, F32(1.0), F32(0.0))
    meta[x_hi, core, :, CAP : CAP + LAT] = jnp.where(named, F32(1.0), F32(0.0))
    own_meta = meta.at[x_hi, core]
    meta_copies = [
        remote(own_meta, own_meta, meta_s.at[i], meta_r.at[i], target)
        for i, target in enumerate((sibling, partner, partner_sibling))
    ]
    for copy in meta_copies:
        copy.start()
    pair.wait_recv()

    chip_rows = pl.ds(pl.multiple_of(y * 16, 16), 16)
    mine = slab_at(x, z)

    def spread(part, low, high):
        both = jnp.concatenate([wide[0, :, low:high], wide[1, :, low:high]], axis=0)
        part[mine, chip_rows, :] = both.astype(BF16)
        for offset in range(1, NY):
            along_y(part, offset).start()

    def along_y(part, offset):
        block = part.at[mine, chip_rows, :]
        return remote(
            block,
            block,
            ring_y_s.at[offset],
            ring_y_r.at[offset],
            device_at(x, (y + offset) % NY, z, core),
        )

    @pl.when(core == 0)
    def _():
        spread(part_a, 0, COLS_A)

    @pl.when(core == 1)
    def _():
        spread(part_b, COLS_A, V)

    for offset in ORDER:
        if offset not in FIRST:
            dispatch(offset).start()
    near[1].wait()

    def pair_slab(t, place):
        return slab_at(x_hi * 2 + (x_lo + t) % 2, place)

    def first(part):
        block = part.at[mine]
        return remote(block, block, first_s, first_r, beside)

    def second(part, k, t, way):
        block = part.at[pair_slab(t, (z - way * k + NZ) % NZ)]
        index = ((way + 1) // 2 * (NZ // 2) + k) * 2 + t
        return remote(
            block,
            block,
            second_s.at[index],
            second_r.at[index],
            device_at(x, y, (z + way + NZ) % NZ, core),
        )

    def swap(part, t, place):
        block = part.at[pair_slab(t, place)]
        index = (x_lo + t) % 2 * NZ + place
        return remote(block, block, swap_s.at[index], swap_r.at[index], sibling)

    def place_of(step):
        return (step + y) % (NZ // 2) * 2 + core

    def head_of(step):
        return 2 * place_of(step) + x_hi

    def clip_cols(side, line):
        return pl.ds(pl.multiple_of(side * 1024 + line * 128, 128), 128)

    def result(step, half, side):
        target = 2 * head_of(step) + half
        copy = remote(
            packed.at[step, side, pl.ds(half * 64, 64), :],
            out.at[:, clip_cols(side, y)],
            out_s.at[(2 * step + half) * 2 + side],
            out_r.at[side * NY + y],
            (group, target),
        )
        return target, copy

    def attend(step):
        head = head_of(step)
        both = jnp.concatenate(
            [
                jnp.concatenate([part_a[head], part_a[16 + head]], axis=0),
                jnp.concatenate([part_b[head], part_b[16 + head]], axis=0),
            ],
            axis=1,
        )
        query = queries[:, pl.ds(pl.multiple_of(head * HD, HD), HD)]
        clips = [(side, i) for side in range(2) for i in range(2)]
        blocks = [nt_dot(both, rows[side, i]).astype(BF16) for side, i in clips]
        scored = [jnp.dot(query, part[:HD], preferred_element_type=F32) for part in blocks]
        weights = [softmax(scored[n], masks[side, i]) for n, (side, i) in enumerate(clips)]
        blended = [nt_dot(blocks[n][HD:], weights[n]) for n in range(4)]
        for side in range(2):
            packed[step, side] = jnp.concatenate(
                blended[2 * side : 2 * side + 2], axis=1
            ).astype(BF16)
        for half in range(2):
            for side in range(2):
                send_result(step, half, side)

    def send_result(step, half, side):
        target, copy = result(step, half, side)

        @pl.when(target == dev)
        def _():
            out[:, clip_cols(side, y)] = packed[step, side, half * 64 : (half + 1) * 64, :]

        @pl.when(target != dev)
        def _():
            copy.start()

    def attend_all(other_part, low, high):
        def one_head(step, carry):
            for t in range(2):
                swap(other_part, t, place_of(step)).wait_recv()
            attend(step)
            return carry

        lax.fori_loop(low, high, one_head, 0)

    def hand_wait(index, carry):
        block = rows_of(x_hi, 0)
        remote(block, block, hand_s.at[index], hand_r.at[index], sibling).wait_recv()
        return carry

    def arrived(offset):
        dispatch(offset).wait_recv()
        cross(offset).start()
        hand_over(0, offset).start()

    def crossed(offset):
        cross(offset).wait_recv()
        hand_over(1, offset).start()

    def run_gather(part, other_part, other):
        state = [0, [], []]

        def move_rows(near_rows, far_rows):
            for offset in near_rows:
                arrived(offset)
            for offset in far_rows:
                crossed(offset)
            for i, new in enumerate((near_rows, far_rows)):
                state[i + 1] += new

        def tick():
            move_rows(*ROWS_AT.get(state[0], ((), ())))
            state[0] += 1

        def landed(t, place):
            @pl.when(place % 2 == other)
            def _():
                swap(part, t, place).start()

        for offset in range(1, NY):
            along_y(part, offset).wait_recv()
        first(part).start()
        for t in range(2):
            if t == 1:
                first(part).wait_recv()
            for way in (1, -1):
                second(part, 0, t, way).start()
            landed(t, z)
            if t == 0:
                tick()
        tick()
        for k in range(1, NZ // 2 + 1):
            for t in range(2):
                for way in (1, -1):
                    chosen = t == (1 - way) // 2
                    if k == NZ // 2 and not chosen:
                        continue
                    second(part, k - 1, t, way).wait_recv()
                    if k < NZ // 2 - 1 or (k == NZ // 2 - 1 and chosen):
                        second(part, k, t, way).start()
                    landed(t, (z - way * k + NZ) % NZ)
                    tick()
        for copy in meta_copies:
            copy.wait_recv()
        for side in range(2):
            for i in range(2):
                masks[side, i] = lax.dot_general(
                    meta[side, i, :, CAP : CAP + LAT],
                    meta[side, i, :, 0:CAP],
                    (((0,), (0,)), ((), ())),
                    preferred_element_type=F32,
                )
        left = [
            tuple(o for o in (0,) + ORDER if o not in done and (i == 1 or o))
            for i, done in enumerate(state[1:])
        ]
        move_rows(*left)
        lax.fori_loop(0, 2 * NY, hand_wait, 0)
        attend_all(other_part, 0, NZ // 2)

    @pl.when(core == 0)
    def _():
        run_gather(part_a, part_b, 1)

    @pl.when(core == 1)
    def _():
        run_gather(part_b, part_a, 0)

    def finish(line, carry):
        source = (y % 2) * 2 * NY + line * 2 + (y // 2) % 2

        @pl.when(source != dev)
        def _():
            for side in range(2):
                remote(
                    packed.at[0, side, pl.ds(0, 64), :],
                    out.at[:, clip_cols(side, line)],
                    out_s.at[0],
                    out_r.at[side * NY + line],
                    sibling,
                ).wait_recv()

        return carry

    lax.fori_loop(0, NY, finish, 0)

    def sent(step, carry):
        for half in range(2):
            for side in range(2):
                target, copy = result(step, half, side)

                @pl.when(target != dev)
                def _():
                    copy.wait_send()

        return carry

    lax.fori_loop(0, NZ // 2, sent, 0)

    pair.wait_send()
    for copy in meta_copies:
        copy.wait_send()

    def sent_rows(offset, carry):
        @pl.when(offset > 0)
        def _():
            dispatch(offset).wait_send()

        cross(offset).wait_send()
        for far in range(2):
            hand_over(far, offset).wait_send()
        return carry

    lax.fori_loop(0, NY, sent_rows, 0)

    def end_gather(part, other):
        for offset in range(1, NY):
            along_y(part, offset).wait_send()
        first(part).wait_send()
        for way in (1, -1):
            for k in range(NZ // 2):
                for t in range(2):
                    if k < NZ // 2 - 1 or t == (1 - way) // 2:
                        second(part, k, t, way).wait_send()
        for t in range(2):
            for place in range(other, NZ, 2):
                swap(part, t, place).wait_send()

    @pl.when(core == 0)
    def _():
        end_gather(part_a, 1)

    @pl.when(core == 1)
    def _():
        end_gather(part_b, 0)


def per_device(
    patches,
    norm_gain,
    kv_weight,
    latent_q,
    clip_frames,
    row_owner,
    row_slot,
    slot_pos,
    latent_blocks,
):
    vmem = pl.BlockSpec(memory_space=pltpu.VMEM)
    far = pl.BlockSpec(memory_space=pltpu.HBM)
    dma = pltpu.SemaphoreType.DMA
    scratch = [
        pltpu.VMEM((32, HD, COLS_A), BF16),
        pltpu.VMEM((32, HD, COLS_B), BF16),
        pltpu.VMEM((2, 2, CAP, V), BF16),
        pltpu.VMEM((2, NY, 2, SLOT, V), BF16),
        pltpu.VMEM((2, 8, V), F32),
        pltpu.VMEM((2, 2, 8, CAP + HD), F32),
        pltpu.VMEM((2, 2, LAT, CAP), F32),
        pltpu.VMEM((4, 2, HD, 2 * LAT), BF16),
        pltpu.VMEM((256, V), BF16),
        pltpu.VMEM((LAT, 2048), BF16),
        dma((2,)),
        dma,
        dma,
        dma((8,)),
        dma((8,)),
        dma,
        dma,
    ]
    for count in (16, 16, 8, 8, 16, 3, 16):
        scratch += [dma((count,)), dma((count,))]
    return pl.pallas_call(
        kernel,
        out_shape=jax.ShapeDtypeStruct((64, 2048), BF16),
        in_specs=[far, vmem, vmem, far] + [vmem] * 5,
        out_specs=vmem,
        scratch_shapes=scratch,
        compiler_params=pltpu.CompilerParams(
            collective_id=0, has_side_effects=True, vmem_limit_bytes=63 * 1024 * 1024
        ),
    )(
        patches[0, 0],
        norm_gain,
        kv_weight,
        latent_q,
        clip_frames,
        row_owner[0],
        row_slot[0],
        slot_pos[0],
        latent_blocks[0, 0].T,
    )


def solution(mesh):
    return jax.shard_map(
        per_device,
        mesh=mesh,
        in_specs=(
            P("group", "dev", None, None),
            P(),
            P(("group", "dev"), None),
            P(),
            P("group", "dev"),
            P("group", "dev", None),
            P("group", "dev", None),
            P("group", "dev", None),
            P("group", "dev", None, None),
        ),
        out_specs=P("dev", "group"),
        check_vma=False,
    )
```

```python
import jax
import jax.numpy as jnp
from jax import lax
from jax.experimental import pallas as pl
from jax.experimental.pallas import tpu as pltpu
from jax.sharding import PartitionSpec as P

HD = 128
LAT = 64
FR_ROWS = 64
V = 1152
COLS_A = 640
COLS_B = 512
CAP = 512
SLOT = 16
NX, NY, NZ = 4, 8, 8
MESH = pl.DeviceIdType.MESH
F32 = jnp.float32
BF16 = jnp.bfloat16


def device_at(x, y, z, core):
    return ((x % 2) * NZ + z, (x // 2) * 2 * NY + y * 2 + core)


def slab_at(x, z):
    return ((x % 2) * NZ + z) * 2 + x // 2


ORDER = (1, 7, 2, 6, 3, 5, 4)
ROWS_AT = {
    0: ((1, 7), ()),
    2: ((), (0,)),
    3: ((2, 6), ()),
    5: ((), (1, 7)),
    7: ((3, 5), ()),
    8: ((), (2, 6)),
    10: ((4,), ()),
    12: ((), (3, 5)),
}
FIRST = (1, 7)


def nt_dot(left, right):
    return lax.dot_general(left, right, (((1,), (1,)), ((), ())), preferred_element_type=F32)


def softmax(scores, mask):
    scores = jnp.where(mask > 0.5, scores * HD ** (-0.5), F32(-1e30))
    raised = jnp.exp(scores - jnp.max(scores, axis=-1, keepdims=True))
    return (raised * (1.0 / jnp.sum(raised, axis=-1, keepdims=True))).astype(BF16)


def remote(src, dst, send_sem, recv_sem, target):
    return pltpu.make_async_remote_copy(
        src_ref=src,
        dst_ref=dst,
        send_sem=send_sem,
        recv_sem=recv_sem,
        device_id=target,
        device_id_type=MESH,
    )


def kernel(
    patches_far,
    gain,
    weight,
    queries_far,
    frames,
    owner,
    slot,
    places,
    listed,
    out,
    part_a,
    part_b,
    rows,
    outbox,
    wide,
    meta,
    masks,
    packed,
    patches,
    queries,
    near_s,
    pair_s,
    pair_r,
    ring_y_s,
    ring_y_r,
    first_s,
    first_r,
    second_s,
    second_r,
    swap_s,
    swap_r,
    send_s,
    send_r,
    cross_s,
    cross_r,
    hand_s,
    hand_r,
    meta_s,
    meta_r,
    out_s,
    out_r,
):
    group = lax.axis_index("group")
    dev = lax.axis_index("dev")
    x_lo, z = group // NZ, group % NZ
    x_hi, in_line = dev // (2 * NY), dev % (2 * NY)
    y, core = in_line // 2, in_line % 2
    x = x_hi * 2 + x_lo
    sibling = (group, x_hi * 2 * NY + y * 2 + 1 - core)
    partner = (group, (1 - x_hi) * 2 * NY + y * 2 + core)
    partner_sibling = (group, (1 - x_hi) * 2 * NY + y * 2 + 1 - core)
    beside = ((1 - x_lo) * NZ + z, dev)

    near = [
        pltpu.make_async_copy(patches_far, patches, near_s.at[0]),
        pltpu.make_async_copy(queries_far, queries, near_s.at[1]),
    ]
    for copy in near:
        copy.start()

    barrier = pltpu.get_barrier_semaphore()

    def greet(offset, carry):
        pl.semaphore_signal(
            barrier, inc=1, device_id=(group, (dev + offset) % 32), device_id_type=MESH
        )
        return carry

    lax.fori_loop(1, 32, greet, 0)
    for target in (
        device_at(x, y, (z + 1) % NZ, core),
        device_at(x, y, (z + NZ - 1) % NZ, core),
        beside,
    ):
        pl.semaphore_signal(barrier, inc=1, device_id=target, device_id_type=MESH)
    own_rows = pl.ds(pl.multiple_of(dev * SLOT, SLOT), SLOT)

    def rows_of(x_hi_from, offset):
        source = x_hi_from * 2 * NY + (y + NY - offset) % NY * 2 + core
        return rows.at[:, :, pl.ds(pl.multiple_of(source * SLOT, SLOT), SLOT), :]

    def dispatch(offset):
        there = (y + offset) % NY
        return remote(
            outbox.at[:, there],
            rows.at[:, :, own_rows, :],
            send_s.at[offset],
            send_r.at[offset],
            (group, x_hi * 2 * NY + there * 2 + core),
        )

    def cross(offset):
        block = rows_of(x_hi, offset)
        return remote(block, block, cross_s.at[offset], cross_r.at[offset], partner)

    def hand_over(far, offset):
        block = rows_of(1 - x_hi if far else x_hi, offset)
        index = far * NY + offset
        return remote(block, block, hand_s.at[index], hand_r.at[index], sibling)

    near[0].wait()
    widened = patches[...].astype(F32)
    inverse_rms = lax.rsqrt(jnp.sum(widened * widened, axis=-1, keepdims=True) * (1.0 / V) + 1e-06)
    normed = (widened * inverse_rms * gain[...].reshape(1, V)).astype(BF16)
    target_slot = owner[...] * SLOT + slot[...]
    onehot = (
        lax.broadcasted_iota(jnp.int32, (CAP, target_slot.shape[1]), 0) == target_slot
    ).astype(F32).astype(BF16)
    outbox[...] = (
        jnp.dot(onehot, normed, preferred_element_type=F32).astype(BF16).reshape(2, NY, 2, SLOT, V)
    )
    rows[:, :, own_rows, :] = outbox[:, y]
    pl.semaphore_wait(barrier, 34)

    cross(0).start()
    hand_over(0, 0).start()
    for offset in FIRST:
        dispatch(offset).start()

    wide[core] = weight[...].astype(F32)
    pair = remote(wide.at[core], wide.at[core], pair_s, pair_r, sibling)
    pair.start()

    position = places[...]
    marks = listed[...]
    block_of = lax.broadcasted_iota(jnp.int32, (8, CAP), 0)
    in_block = (block_of == position // (2 * FR_ROWS)) & (position < frames[...] * FR_ROWS)
    named = lax.broadcasted_iota(jnp.int32, (8, LAT), 0)
    named = (named == marks[0:1, :]) | (named == marks[1:2, :])
    meta[x_hi, core, :, 0:CAP] = jnp.where(in_block, F32(1.0), F32(0.0))
    meta[x_hi, core, :, CAP : CAP + LAT] = jnp.where(named, F32(1.0), F32(0.0))
    own_meta = meta.at[x_hi, core]
    meta_copies = [
        remote(own_meta, own_meta, meta_s.at[i], meta_r.at[i], target)
        for i, target in enumerate((sibling, partner, partner_sibling))
    ]
    for copy in meta_copies:
        copy.start()
    pair.wait_recv()

    chip_rows = pl.ds(pl.multiple_of(y * 16, 16), 16)
    mine = slab_at(x, z)

    def spread(part, low, high):
        both = jnp.concatenate([wide[0, :, low:high], wide[1, :, low:high]], axis=0)
        part[mine, chip_rows, :] = both.astype(BF16)
        for offset in range(1, NY):
            along_y(part, offset).start()

    def along_y(part, offset):
        block = part.at[mine, chip_rows, :]
        return remote(
            block,
            block,
            ring_y_s.at[offset],
            ring_y_r.at[offset],
            device_at(x, (y + offset) % NY, z, core),
        )

    @pl.when(core == 0)
    def _():
        spread(part_a, 0, COLS_A)

    @pl.when(core == 1)
    def _():
        spread(part_b, COLS_A, V)

    for offset in ORDER:
        if offset not in FIRST:
            dispatch(offset).start()
    near[1].wait()

    def pair_slab(t, place):
        return slab_at(x_hi * 2 + (x_lo + t) % 2, place)

    def first(part):
        block = part.at[mine]
        return remote(block, block, first_s, first_r, beside)

    def second(part, k, t, way):
        block = part.at[pair_slab(t, (z - way * k + NZ) % NZ)]
        index = ((way + 1) // 2 * (NZ // 2) + k) * 2 + t
        return remote(
            block,
            block,
            second_s.at[index],
            second_r.at[index],
            device_at(x, y, (z + way + NZ) % NZ, core),
        )

    def swap(part, t, place):
        block = part.at[pair_slab(t, place)]
        index = (x_lo + t) % 2 * NZ + place
        return remote(block, block, swap_s.at[index], swap_r.at[index], sibling)

    def place_of(step):
        return (step + y) % (NZ // 2) * 2 + core

    def head_of(step):
        return 2 * place_of(step) + x_hi

    def clip_cols(side, line):
        return pl.ds(pl.multiple_of(side * 1024 + line * 128, 128), 128)

    def result(step, half, side):
        target = 2 * head_of(step) + half
        copy = remote(
            packed.at[step, side, pl.ds(half * 64, 64), :],
            out.at[:, clip_cols(side, y)],
            out_s.at[(2 * step + half) * 2 + side],
            out_r.at[side * NY + y],
            (group, target),
        )
        return target, copy

    def attend(step):
        head = head_of(step)
        both = jnp.concatenate(
            [
                jnp.concatenate([part_a[head], part_a[16 + head]], axis=0),
                jnp.concatenate([part_b[head], part_b[16 + head]], axis=0),
            ],
            axis=1,
        )
        query = queries[:, pl.ds(pl.multiple_of(head * HD, HD), HD)]
        clips = [(side, i) for side in range(2) for i in range(2)]
        blocks = [nt_dot(both, rows[side, i]).astype(BF16) for side, i in clips]
        scored = [jnp.dot(query, part[:HD], preferred_element_type=F32) for part in blocks]
        weights = [softmax(scored[n], masks[side, i]) for n, (side, i) in enumerate(clips)]
        blended = [nt_dot(blocks[n][HD:], weights[n]) for n in range(4)]
        for side in range(2):
            packed[step, side] = jnp.concatenate(
                blended[2 * side : 2 * side + 2], axis=1
            ).astype(BF16)
        for half in range(2):
            for side in range(2):
                send_result(step, half, side)

    def send_result(step, half, side):
        target, copy = result(step, half, side)

        @pl.when(target == dev)
        def _():
            out[:, clip_cols(side, y)] = packed[step, side, half * 64 : (half + 1) * 64, :]

        @pl.when(target != dev)
        def _():
            copy.start()

    def attend_all(other_part, low, high):
        def one_head(step, carry):
            for t in range(2):
                swap(other_part, t, place_of(step)).wait_recv()
            attend(step)
            return carry

        lax.fori_loop(low, high, one_head, 0)

    def hand_wait(index, carry):
        block = rows_of(x_hi, 0)
        remote(block, block, hand_s.at[index], hand_r.at[index], sibling).wait_recv()
        return carry

    def arrived(offset):
        dispatch(offset).wait_recv()
        cross(offset).start()
        hand_over(0, offset).start()

    def crossed(offset):
        cross(offset).wait_recv()
        hand_over(1, offset).start()

    def run_gather(part, other_part, other):
        state = [0, [], []]

        def move_rows(near_rows, far_rows):
            for offset in near_rows:
                arrived(offset)
            for offset in far_rows:
                crossed(offset)
            for i, new in enumerate((near_rows, far_rows)):
                state[i + 1] += new

        def tick():
            move_rows(*ROWS_AT.get(state[0], ((), ())))
            state[0] += 1

        def landed(t, place):
            @pl.when(place % 2 == other)
            def _():
                swap(part, t, place).start()

        for offset in range(1, NY):
            along_y(part, offset).wait_recv()
        first(part).start()
        for t in range(2):
            if t == 1:
                first(part).wait_recv()
            for way in (1, -1):
                second(part, 0, t, way).start()
            landed(t, z)
            if t == 0:
                tick()
        tick()
        for k in range(1, NZ // 2 + 1):
            for t in range(2):
                for way in (1, -1):
                    chosen = t == (1 - way) // 2
                    if k == NZ // 2 and not chosen:
                        continue
                    second(part, k - 1, t, way).wait_recv()
                    if k < NZ // 2 - 1 or (k == NZ // 2 - 1 and chosen):
                        second(part, k, t, way).start()
                    landed(t, (z - way * k + NZ) % NZ)
                    tick()
        for copy in meta_copies:
            copy.wait_recv()
        for side in range(2):
            for i in range(2):
                masks[side, i] = lax.dot_general(
                    meta[side, i, :, CAP : CAP + LAT],
                    meta[side, i, :, 0:CAP],
                    (((0,), (0,)), ((), ())),
                    preferred_element_type=F32,
                )
        left = [
            tuple(o for o in (0,) + ORDER if o not in done and (i == 1 or o))
            for i, done in enumerate(state[1:])
        ]
        move_rows(*left)
        lax.fori_loop(0, 2 * NY, hand_wait, 0)
        attend_all(other_part, 0, NZ // 2)

    @pl.when(core == 0)
    def _():
        run_gather(part_a, part_b, 1)

    @pl.when(core == 1)
    def _():
        run_gather(part_b, part_a, 0)

    def finish(line, carry):
        source = (y % 2) * 2 * NY + line * 2 + (y // 2) % 2

        @pl.when(source != dev)
        def _():
            for side in range(2):
                remote(
                    packed.at[0, side, pl.ds(0, 64), :],
                    out.at[:, clip_cols(side, line)],
                    out_s.at[0],
                    out_r.at[side * NY + line],
                    sibling,
                ).wait_recv()

        return carry

    lax.fori_loop(0, NY, finish, 0)

    def sent(step, carry):
        for half in range(2):
            for side in range(2):
                target, copy = result(step, half, side)

                @pl.when(target != dev)
                def _():
                    copy.wait_send()

        return carry

    lax.fori_loop(0, NZ // 2, sent, 0)

    pair.wait_send()
    for copy in meta_copies:
        copy.wait_send()

    def sent_rows(offset, carry):
        @pl.when(offset > 0)
        def _():
            dispatch(offset).wait_send()

        cross(offset).wait_send()
        for far in range(2):
            hand_over(far, offset).wait_send()
        return carry

    lax.fori_loop(0, NY, sent_rows, 0)

    def end_gather(part, other):
        for offset in range(1, NY):
            along_y(part, offset).wait_send()
        first(part).wait_send()
        for way in (1, -1):
            for k in range(NZ // 2):
                for t in range(2):
                    if k < NZ // 2 - 1 or t == (1 - way) // 2:
                        second(part, k, t, way).wait_send()
        for t in range(2):
            for place in range(other, NZ, 2):
                swap(part, t, place).wait_send()

    @pl.when(core == 0)
    def _():
        end_gather(part_a, 1)

    @pl.when(core == 1)
    def _():
        end_gather(part_b, 0)


def per_device(
    patches,
    norm_gain,
    kv_weight,
    latent_q,
    clip_frames,
    row_owner,
    row_slot,
    slot_pos,
    latent_blocks,
):
    vmem = pl.BlockSpec(memory_space=pltpu.VMEM)
    far = pl.BlockSpec(memory_space=pltpu.HBM)
    dma = pltpu.SemaphoreType.DMA
    scratch = [
        pltpu.VMEM((32, HD, COLS_A), BF16),
        pltpu.VMEM((32, HD, COLS_B), BF16),
        pltpu.VMEM((2, 2, CAP, V), BF16),
        pltpu.VMEM((2, NY, 2, SLOT, V), BF16),
        pltpu.VMEM((2, 8, V), F32),
        pltpu.VMEM((2, 2, 8, CAP + HD), F32),
        pltpu.VMEM((2, 2, LAT, CAP), F32),
        pltpu.VMEM((4, 2, HD, 2 * LAT), BF16),
        pltpu.VMEM((256, V), BF16),
        pltpu.VMEM((LAT, 2048), BF16),
        dma((2,)),
        dma,
        dma,
        dma((8,)),
        dma((8,)),
        dma,
        dma,
    ]
    for count in (16, 16, 8, 8, 16, 3, 16):
        scratch += [dma((count,)), dma((count,))]
    return pl.pallas_call(
        kernel,
        out_shape=jax.ShapeDtypeStruct((64, 2048), BF16),
        in_specs=[far, vmem, vmem, far] + [vmem] * 5,
        out_specs=vmem,
        scratch_shapes=scratch,
        compiler_params=pltpu.CompilerParams(
            collective_id=0, has_side_effects=True, vmem_limit_bytes=63 * 1024 * 1024
        ),
    )(
        patches[0, 0],
        norm_gain,
        kv_weight,
        latent_q,
        clip_frames,
        row_owner[0],
        row_slot[0],
        slot_pos[0],
        latent_blocks[0, 0].T,
    )


def solution(mesh):
    return jax.shard_map(
        per_device,
        mesh=mesh,
        in_specs=(
            P("group", "dev", None, None),
            P(),
            P(("group", "dev"), None),
            P(),
            P("group", "dev"),
            P("group", "dev", None),
            P("group", "dev", None),
            P("group", "dev", None),
            P("group", "dev", None, None),
        ),
        out_specs=P("dev", "group"),
        check_vma=False,
    )
```
